512 devices in a mesh: group: 2 (over z_lo), dp: 32 (over z_hi, y), tensor: 8 (over x, core).
Axes of the slice: x: 4, y: 8, z: 8 (z_hi: 4, z_lo: 2; z = z_hi * 2 + z_lo), core: 2. Of those that a mesh axis runs over, the one named last changes fastest.
Arguments:
- teacher_stream: float32 [8192, 6144], P('dp', ('group', 'tensor')), may hold values from -1100 to 1100
- teacher_gain: float32 [6144], P(('group', 'tensor')), may hold values from 0.25 to 1.75
- projection: bfloat16 [6144, 4096], P('dp', ('group', 'tensor')), may hold values from -0.078125 to 0.078125
- student_stream: float32 [8192, 4096], P('dp', ('group', 'tensor')), may hold values from -1100 to 1100
- student_context: bfloat16 [8192, 4096], P('dp', ('group', 'tensor')), may hold values from -12 to 12
- out_weight: bfloat16 [4096, 4096], P('dp', ('group', 'tensor')), may hold values from -0.09375 to 0.09375
- student_gain: float32 [4096], P(('group', 'tensor')), may hold values from 0.25 to 1.75
Outputs:
- student_out: float32 [8192, 4096], P('dp', ('group', 'tensor'))
- weight_grad: float32 [4096, 4096], P('dp', ('group', 'tensor'))
The draws below stay inside these ranges and needn't reach their ends.
All inputs are finite; a program needn't handle non-finite values.
Results may differ from the reference program's by a relative error of at most 0.004.
Values may be sent and summed in bfloat16 or wider, within the bound.
No kernel may reach another device: no remote copies, remote signals or barrier semaphores. Data moves between devices by JAX's collectives and lax.ppermute only.
A program may use at most 64 MiB of HBM per device.

```python
import math
import jax
import jax.numpy as jnp
from jax import lax

DT = 6144
DS = 4096
TOKENS = 8192


def field(jitter, level_key, growth, spread):
    row_count = jitter.shape[0]
    col_count = jitter.shape[1]
    position = jnp.arange(col_count, dtype=jnp.float32) / (col_count - 1)
    columns = growth ** position
    levels = spread ** jax.random.uniform(level_key, (row_count, 1), jnp.float32)
    return levels * columns * (0.5 + jitter)


def draw_teacher_stream(key, part):
    key = jax.random.fold_in(key, 7)
    jitter_key, level_key = jax.random.split(key)
    jitter = jnp.clip(jax.random.normal(jitter_key, (TOKENS, DT), jnp.float32), -4.0, 4.0)
    return field(jitter, level_key, 10.0, 10.0)


def draw_student_stream(key, part):
    key = jax.random.fold_in(key, 9)
    jitter_key, level_key = jax.random.split(key)
    jitter = jnp.clip(jax.random.normal(jitter_key, (TOKENS, DS), jnp.float32), -4.0, 4.0)
    return field(jitter, level_key, 10.0, 10.0)


def shard_levels(own_key, dims, pieces, smallest, largest):
    level, own = 1.0, jax.random.fold_in(own_key, 6)
    for dim, parts in pieces:
        draws = jnp.exp(jax.random.uniform(jax.random.fold_in(own, dim), (parts,), jnp.float32, smallest / len(pieces), largest / len(pieces)))
        level = level * jnp.repeat(draws, dims[dim] // parts).reshape([-1 if axis == dim else 1 for axis in range(len(dims))])
    return level


def gaussian(key, extent, scale, bound, cuts=(), kind=jnp.bfloat16):
    factor_of = shard_levels(key, extent, cuts, -0.22, 0.18) if cuts else 1.0
    values = jax.random.normal(key, extent, jnp.float32) * scale * factor_of
    return jnp.minimum(jnp.maximum(values, -bound), bound).astype(kind)


def setup_inputs(seed: int = 0) -> dict:
    streams_of = jax.random.split(jax.random.key(seed), 8)
    teacher_stream = draw_teacher_stream(jax.random.fold_in(streams_of[7], 71), 0)
    teacher_gain = jnp.clip(1.0 + 0.15 * jax.random.normal(streams_of[1], (DT,), jnp.float32), 0.25, 1.75)
    projection = gaussian(streams_of[2], (DT, DS), DT ** -0.5, 0.078125, ((0, 32), (1, 16)))
    student_stream = draw_student_stream(jax.random.fold_in(streams_of[7], 71), 0)
    student_context = gaussian(streams_of[4], (TOKENS, DS), 2.0, 12.0, ((0, 32), (1, 16)))
    out_weight = gaussian(streams_of[5], (DS, DS), DS ** -0.5, 0.09375, ((0, 32), (1, 16)))
    student_gain = jnp.clip(1.0 + 0.15 * jax.random.normal(streams_of[6], (DS,), jnp.float32), 0.25, 1.75)
    return dict(teacher_stream=teacher_stream, teacher_gain=teacher_gain, projection=projection, student_stream=student_stream, student_context=student_context, out_weight=out_weight, student_gain=student_gain)


EPSILON = 1e-05

def normalize(values):
    row_mean = lax.optimization_barrier(jnp.mean(values, axis=-1, keepdims=True))
    centered = values - row_mean
    row_var = lax.optimization_barrier(jnp.mean(centered * centered, axis=-1, keepdims=True))
    inv_std = lax.rsqrt(row_var + EPSILON)
    return (centered * inv_std, inv_std)

def reference(teacher_stream, teacher_gain, projection, student_stream, student_context, out_weight, student_gain):
    teacher_norm, _ = normalize(teacher_stream)
    teacher_hidden = (teacher_norm * teacher_gain).astype(jnp.bfloat16)
    target = jnp.dot(teacher_hidden, projection, preferred_element_type=jnp.float32)
    pre_norm = student_stream + jnp.dot(student_context, out_weight, preferred_element_type=jnp.float32)
    normalized, inv_std = normalize(pre_norm)
    student_out = normalized * student_gain
    scaled = (student_out - target) * (1.0 / math.sqrt(TOKENS))
    grad_norm = scaled * student_gain
    first_mean = lax.optimization_barrier(jnp.mean(grad_norm, axis=-1, keepdims=True))
    second_mean = lax.optimization_barrier(jnp.mean(grad_norm * normalized, axis=-1, keepdims=True))
    grad_pre = (inv_std * (grad_norm - first_mean - normalized * second_mean)).astype(jnp.bfloat16)
    weight_grad = jnp.dot(student_context.T, grad_pre, preferred_element_type=jnp.float32)
    return (student_out, weight_grad)
```

```python
import math

import jax
import jax.numpy as jnp
from jax import lax
from jax.sharding import Mesh, PartitionSpec as P

EPSILON = 1e-05
BF16 = jnp.bfloat16
F32 = jnp.float32

TOKEN_AXES = ("zhigh", "yhigh", "row")
GATHER_AXES = ("zhigh", "yhigh")
FEATURE_AXES = ("group", "x", "core")


def swap(values, axis):
    return lax.ppermute(values, axis, [(0, 1), (1, 0)])


def ordered(mine, other, place, axis):
    first = place == 0
    return jnp.concatenate(
        [jnp.where(first, mine, other), jnp.where(first, other, mine)], axis=axis
    )


def my_half(values, place):
    half = values.shape[1] // 2
    return (
        jnp.where(place == 0, values[:, :half], values[:, half:]),
        jnp.where(place == 0, values[:, half:], values[:, :half]),
    )


def split_tokens(values, row):
    keep, give = my_half(values, row)
    return jnp.concatenate([keep, swap(give, "row")], axis=0)


def gather_line(values):
    count = lax.axis_size("x")
    place = lax.axis_index("x")
    ahead = [(i, (i + 1) % count) for i in range(count)]
    back = [(i, (i - 1) % count) for i in range(count)]
    rows = values.shape[0] // 2
    previous = lax.ppermute(values, "x", ahead)
    following = lax.ppermute(values, "x", back)
    opposite = jnp.concatenate(
        [
            lax.ppermute(previous[:rows], "x", ahead),
            lax.ppermute(following[rows:], "x", back),
        ],
        axis=0,
    )
    pieces = [values, previous, opposite, following]
    return jnp.concatenate(
        [lax.select_n((place - j) & (count - 1), *pieces) for j in range(count)], axis=1
    )


def gather_features(values):
    pair = ordered(values, swap(values, "group"), lax.axis_index("group"), 1)
    line = gather_line(pair)
    return line, swap(line, "core")


def both(first, place):
    return (
        jnp.where(place == 0, first[0], first[1]),
        jnp.where(place == 0, first[1], first[0]),
    )


def product(pair, weight_pair):
    return jnp.dot(pair[0], weight_pair[0], preferred_element_type=F32) + jnp.dot(
        pair[1], weight_pair[1], preferred_element_type=F32
    )


def moments(values):
    mean = jnp.mean(values, axis=1)
    centered = values - mean[:, None]
    return mean, centered, jnp.sum(centered * centered, axis=1)


def combine(means, squares, width):
    mean = jnp.mean(means, axis=0)
    shift = means - mean
    variance = jnp.mean(squares / width + shift * shift, axis=0)
    return mean, shift, lax.rsqrt(variance + EPSILON)


def gather_rows(rows):
    return lax.all_gather(jnp.stack(rows, axis=0), FEATURE_AXES, axis=0)


def shards(
    teacher_stream,
    teacher_gain,
    projection,
    student_stream,
    student_context,
    out_weight,
    student_gain,
):
    row = lax.axis_index("row")
    groups, lanes, cores = (lax.axis_size(name) for name in FEATURE_AXES)
    blocks = groups * lanes * cores
    tokens = teacher_stream.shape[0]
    token_count = tokens * lax.axis_size(TOKEN_AXES)
    width = student_stream.shape[1]
    depth = out_weight.shape[0]

    weights = lax.all_gather(
        jnp.concatenate([out_weight, projection], axis=0), GATHER_AXES, axis=0
    )
    weights = weights.reshape(groups, lanes, cores, *weights.shape[1:])
    weights = weights.transpose(2, 1, 0, 3, 4)
    core = lax.axis_index("core")
    out_full = both(weights[:, :, :, :depth].reshape(cores, -1, width), core)
    projection_full = both(weights[:, :, :, depth:].reshape(cores, -1, width), core)

    context = gather_features(split_tokens(student_context, row))

    teacher_mean, _, teacher_square = moments(teacher_stream)
    table = gather_rows([teacher_mean, teacher_square])
    mean, _, inv_std = combine(table[:, 0], table[:, 1], teacher_stream.shape[1])
    hidden = ((teacher_stream - mean[:, None]) * inv_std[:, None] * teacher_gain).astype(BF16)
    hidden = gather_features(split_tokens(hidden, row))

    branch = product(context, out_full)
    pre_norm = student_stream + (branch[:tokens] + swap(branch[tokens:].astype(BF16), "row").astype(F32))
    target = product(hidden, projection_full)
    target = target[:tokens] + swap(target[tokens:].astype(BF16), "row").astype(F32)

    block_mean, centered, square = moments(pre_norm)
    gain_square = student_gain * student_gain
    weighted = centered * gain_square
    scaled_target = target * student_gain
    table = gather_rows(
        [
            block_mean,
            square,
            jnp.sum(weighted, axis=1),
            jnp.sum(weighted * centered, axis=1),
            jnp.sum(scaled_target, axis=1),
            jnp.sum(scaled_target * centered, axis=1),
            jnp.full((tokens,), jnp.sum(gain_square), F32),
        ]
    )
    mean, shift, inv_std = combine(table[:, 0], table[:, 1], width)
    gains = table[:, 6]
    linear = jnp.sum(table[:, 2] + shift * gains, axis=0)
    quadratic = jnp.sum(table[:, 3] + shift * (2.0 * table[:, 2] + shift * gains), axis=0)
    target_sum = jnp.sum(table[:, 4], axis=0)
    target_cross = jnp.sum(table[:, 5] + shift * table[:, 4], axis=0)
    count = width * blocks
    scale = 1.0 / math.sqrt(token_count)
    first_mean = (inv_std * linear - target_sum) * (scale / count)
    second_mean = (inv_std * inv_std * quadratic - inv_std * target_cross) * (scale / count)

    normalized = (pre_norm - mean[:, None]) * inv_std[:, None]
    student_out = normalized * student_gain
    grad_norm = (student_out - target) * scale * student_gain
    grad_pre = (
        inv_std[:, None] * (grad_norm - first_mean[:, None] - normalized * second_mean[:, None])
    ).astype(BF16)
    grad_pre = jnp.concatenate([grad_pre, swap(grad_pre, "row")], axis=0)

    partial = [
        lax.dot_general(
            half, grad_pre, (((0,), (0,)), ((), ())), preferred_element_type=F32
        ).astype(BF16)
        for half in context
    ]
    partial = jnp.stack(both(partial, core), axis=0)
    partial = partial.reshape(cores, lanes, groups, depth, width).transpose(2, 1, 0, 3, 4)
    parts = lax.all_to_all(partial.reshape(blocks, depth, width), GATHER_AXES, 0, 0, tiled=True)
    weight_grad = jnp.sum(parts.astype(F32), axis=0)
    return (student_out, weight_grad)


def solution(mesh):
    groups, token_blocks, columns = (mesh.shape[name] for name in ("group", "dp", "tensor"))
    cores = 2
    zhigh = min(4, token_blocks // 4)
    fine = Mesh(
        mesh.devices.reshape(
            groups, zhigh, token_blocks // (2 * zhigh), 2, columns // cores, cores
        ),
        ("group", "zhigh", "yhigh", "row", "x", "core"),
    )
    split = P(TOKEN_AXES, FEATURE_AXES)
    return jax.shard_map(
        shards,
        mesh=fine,
        in_specs=(
            split,
            P(FEATURE_AXES),
            split,
            split,
            split,
            split,
            P(FEATURE_AXES),
        ),
        out_specs=(split, split),
        check_vma=False,
    )
```

```python
import math

import jax
import jax.numpy as jnp
from jax import lax
from jax.sharding import Mesh, PartitionSpec as P

EPSILON = 1e-05
BF16 = jnp.bfloat16
F32 = jnp.float32

TOKEN_AXES = ("zhigh", "yhigh", "row")
GATHER_AXES = ("zhigh", "yhigh")
FEATURE_AXES = ("group", "x", "core")


def swap(values, axis):
    return lax.ppermute(values, axis, [(0, 1), (1, 0)])


def my_half(values, place):
    half = values.shape[1] // 2
    return (
        jnp.where(place == 0, values[:, :half], values[:, half:]),
        jnp.where(place == 0, values[:, half:], values[:, :half]),
    )


def split_tokens(values, row):
    keep, give = my_half(values, row)
    return jnp.concatenate([keep, swap(give, "row")], axis=0)


def gather_features(values):
    axes = ("group", "x")
    count = lax.axis_size(axes)
    copies = jnp.broadcast_to(values[None], (count, *values.shape))
    line = lax.all_to_all(copies, axes, 0, 0, tiled=True)
    other = swap(line, "core")
    return tuple(
        part.transpose(1, 0, 2).reshape(values.shape[0], -1) for part in (line, other)
    )


def both(first, place):
    return (
        jnp.where(place == 0, first[0], first[1]),
        jnp.where(place == 0, first[1], first[0]),
    )


def product(pair, weight_pair):
    return jnp.dot(pair[0], weight_pair[0], preferred_element_type=F32) + jnp.dot(
        pair[1], weight_pair[1], preferred_element_type=F32
    )


def moments(values):
    mean = jnp.mean(values, axis=1)
    centered = values - mean[:, None]
    return mean, centered, jnp.sum(centered * centered, axis=1)


def combine(means, squares, width):
    mean = jnp.mean(means, axis=0)
    shift = means - mean
    variance = jnp.mean(squares / width + shift * shift, axis=0)
    return mean, shift, lax.rsqrt(variance + EPSILON)


def gather_rows(rows):
    return lax.all_gather(jnp.stack(rows, axis=0), FEATURE_AXES, axis=0)


def shards(
    teacher_stream,
    teacher_gain,
    projection,
    student_stream,
    student_context,
    out_weight,
    student_gain,
):
    row = lax.axis_index("row")
    groups, lanes, cores = (lax.axis_size(name) for name in FEATURE_AXES)
    blocks = groups * lanes * cores
    tokens = teacher_stream.shape[0]
    token_count = tokens * lax.axis_size(TOKEN_AXES)
    width = student_stream.shape[1]
    depth = out_weight.shape[0]

    weights = lax.all_gather(
        jnp.concatenate([out_weight, projection], axis=0), GATHER_AXES, axis=0
    )
    weights = weights.reshape(groups, lanes, cores, *weights.shape[1:])
    weights = weights.transpose(2, 0, 1, 3, 4)
    core = lax.axis_index("core")
    out_full = both(weights[:, :, :, :depth].reshape(cores, -1, width), core)
    projection_full = both(weights[:, :, :, depth:].reshape(cores, -1, width), core)

    context = gather_features(split_tokens(student_context, row))

    teacher_mean, _, teacher_square = moments(teacher_stream)
    table = gather_rows([teacher_mean, teacher_square])
    mean, _, inv_std = combine(table[:, 0], table[:, 1], teacher_stream.shape[1])
    hidden = ((teacher_stream - mean[:, None]) * inv_std[:, None] * teacher_gain).astype(BF16)
    hidden = gather_features(split_tokens(hidden, row))

    branch = product(context, out_full)
    pre_norm = student_stream + (branch[:tokens] + swap(branch[tokens:].astype(BF16), "row").astype(F32))
    target = product(hidden, projection_full)
    target = target[:tokens] + swap(target[tokens:].astype(BF16), "row").astype(F32)

    block_mean, centered, square = moments(pre_norm)
    gain_square = student_gain * student_gain
    weighted = centered * gain_square
    scaled_target = target * student_gain
    table = gather_rows(
        [
            block_mean,
            square,
            jnp.sum(weighted, axis=1),
            jnp.sum(weighted * centered, axis=1),
            jnp.sum(scaled_target, axis=1),
            jnp.sum(scaled_target * centered, axis=1),
            jnp.full((tokens,), jnp.sum(gain_square), F32),
        ]
    )
    mean, shift, inv_std = combine(table[:, 0], table[:, 1], width)
    gains = table[:, 6]
    linear = jnp.sum(table[:, 2] + shift * gains, axis=0)
    quadratic = jnp.sum(table[:, 3] + shift * (2.0 * table[:, 2] + shift * gains), axis=0)
    target_sum = jnp.sum(table[:, 4], axis=0)
    target_cross = jnp.sum(table[:, 5] + shift * table[:, 4], axis=0)
    count = width * blocks
    scale = 1.0 / math.sqrt(token_count)
    first_mean = (inv_std * linear - target_sum) * (scale / count)
    second_mean = (inv_std * inv_std * quadratic - inv_std * target_cross) * (scale / count)

    normalized = (pre_norm - mean[:, None]) * inv_std[:, None]
    student_out = normalized * student_gain
    grad_norm = (student_out - target) * scale * student_gain
    grad_pre = (
        inv_std[:, None] * (grad_norm - first_mean[:, None] - normalized * second_mean[:, None])
    ).astype(BF16)
    grad_pre = jnp.concatenate([grad_pre, swap(grad_pre, "row")], axis=0)

    partial = [
        lax.dot_general(
            half, grad_pre, (((0,), (0,)), ((), ())), preferred_element_type=F32
        ).astype(BF16)
        for half in context
    ]
    partial = jnp.stack(both(partial, core), axis=0)
    partial = partial.reshape(cores, groups, lanes, depth, width).transpose(1, 2, 0, 3, 4)
    parts = lax.all_to_all(partial.reshape(blocks, depth, width), GATHER_AXES, 0, 0, tiled=True)
    weight_grad = jnp.sum(parts.astype(F32), axis=0)
    return (student_out, weight_grad)


def solution(mesh):
    groups, token_blocks, columns = (mesh.shape[name] for name in ("group", "dp", "tensor"))
    cores = 2
    zhigh = min(4, token_blocks // 4)
    fine = Mesh(
        mesh.devices.reshape(
            groups, zhigh, token_blocks // (2 * zhigh), 2, columns // cores, cores
        ),
        ("group", "zhigh", "yhigh", "row", "x", "core"),
    )
    split = P(TOKEN_AXES, FEATURE_AXES)
    return jax.shard_map(
        shards,
        mesh=fine,
        in_specs=(
            split,
            P(FEATURE_AXES),
            split,
            split,
            split,
            split,
            P(FEATURE_AXES),
        ),
        out_specs=(split, split),
        check_vma=False,
    )
```

```python
import math

import jax
import jax.numpy as jnp
from jax import lax
from jax.sharding import Mesh, PartitionSpec as P

EPSILON = 1e-05
BF16 = jnp.bfloat16
F32 = jnp.float32

TOKEN_AXES = ("zhigh", "pair", "y")
GATHER_AXES = ("zhigh", "y")
FEATURE_AXES = ("group", "xhigh", "xlow", "core")
CHIP_AXES = ("group", "xhigh", "xlow")


def swap(values, axis):
    return lax.ppermute(values, axis, [(0, 1), (1, 0)])


def turned(values):
    return lax.ppermute(values, ("pair", "xhigh"), [(0, 0), (1, 2), (2, 1), (3, 3)])


def gather_features(values, after=None):
    tokens, width = values.shape
    count = lax.axis_size(CHIP_AXES)
    copies = jnp.broadcast_to(values[None], (count, tokens, width))
    line = lax.all_to_all(copies, CHIP_AXES, 0, 0, tiled=True)
    if after is not None:
        line, after = lax.optimization_barrier((line, after))
    other = swap(line, "core")
    shape = (lax.axis_size("group"), 2, lax.axis_size("xlow"), tokens, width)
    gathered = tuple(
        part.reshape(shape).transpose(1, 3, 0, 2, 4).reshape(2 * tokens, -1)
        for part in (line, other)
    )
    return gathered, after


def both(first, place):
    return (
        jnp.where(place == 0, first[0], first[1]),
        jnp.where(place == 0, first[1], first[0]),
    )


def product(pair, weight_pair):
    return jnp.dot(pair[0], weight_pair[0], preferred_element_type=F32) + jnp.dot(
        pair[1], weight_pair[1], preferred_element_type=F32
    )


def moments(values):
    mean = jnp.mean(values, axis=1)
    centered = values - mean[:, None]
    return mean, centered, jnp.sum(centered * centered, axis=1)


def combine(means, squares, width):
    mean = jnp.mean(means, axis=0)
    shift = means - mean
    variance = jnp.mean(squares / width + shift * shift, axis=0)
    return mean, shift, lax.rsqrt(variance + EPSILON)


def gather_rows(rows):
    return lax.all_gather(jnp.stack(rows, axis=0), FEATURE_AXES, axis=0)


def shards(
    teacher_stream,
    teacher_gain,
    projection,
    student_stream,
    student_context,
    out_weight,
    student_gain,
):
    pair = lax.axis_index("pair")
    core = lax.axis_index("core")
    groups, lanes, cores = (lax.axis_size(name) for name in ("group", "xlow", "core"))
    blocks = lax.axis_size(FEATURE_AXES)
    tokens = teacher_stream.shape[0]
    token_count = tokens * lax.axis_size(TOKEN_AXES)
    width = student_stream.shape[1]
    depth = out_weight.shape[0]

    weights = lax.all_gather(
        jnp.concatenate([out_weight, projection], axis=0), GATHER_AXES, axis=0
    )
    context = turned(student_context)
    teacher_mean, _, teacher_square = moments(teacher_stream)
    table = gather_rows([teacher_mean, teacher_square])
    context, table = lax.optimization_barrier((context, table))
    mean, _, inv_std = combine(table[:, 0], table[:, 1], teacher_stream.shape[1])
    hidden = ((teacher_stream - mean[:, None]) * inv_std[:, None] * teacher_gain).astype(BF16)
    context, _ = gather_features(context)
    hidden, weights = gather_features(turned(hidden), weights)

    weights = weights.reshape(groups, lanes, cores, 2, *weights.shape[1:])
    weights = weights.transpose(2, 0, 1, 3, 4, 5)
    out_full = both(weights[..., :depth, :].reshape(cores, -1, width), core)
    projection_full = both(weights[..., depth:, :].reshape(cores, -1, width), core)

    def shared(partial):
        mine, other = both(partial.reshape(2, tokens, width), pair)
        return mine + swap(other.astype(BF16), "pair").astype(F32)

    pre_norm = student_stream + shared(product(context, out_full))
    target = shared(product(hidden, projection_full))

    block_mean, centered, square = moments(pre_norm)
    gain_square = student_gain * student_gain
    weighted = centered * gain_square
    scaled_target = target * student_gain
    table = gather_rows(
        [
            block_mean,
            square,
            jnp.sum(weighted, axis=1),
            jnp.sum(weighted * centered, axis=1),
            jnp.sum(scaled_target, axis=1),
            jnp.sum(scaled_target * centered, axis=1),
            jnp.full((tokens,), jnp.sum(gain_square), F32),
        ]
    )
    mean, shift, inv_std = combine(table[:, 0], table[:, 1], width)
    gains = table[:, 6]
    linear = jnp.sum(table[:, 2] + shift * gains, axis=0)
    quadratic = jnp.sum(table[:, 3] + shift * (2.0 * table[:, 2] + shift * gains), axis=0)
    target_sum = jnp.sum(table[:, 4], axis=0)
    target_cross = jnp.sum(table[:, 5] + shift * table[:, 4], axis=0)
    count = width * blocks
    scale = 1.0 / math.sqrt(token_count)
    first_mean = (inv_std * linear - target_sum) * (scale / count)
    second_mean = (inv_std * inv_std * quadratic - inv_std * target_cross) * (scale / count)

    normalized = (pre_norm - mean[:, None]) * inv_std[:, None]
    student_out = normalized * student_gain
    grad_norm = (student_out - target) * scale * student_gain
    grad_pre = (
        inv_std[:, None] * (grad_norm - first_mean[:, None] - normalized * second_mean[:, None])
    ).astype(BF16)
    grad_pre = jnp.concatenate(both((grad_pre, swap(grad_pre, "pair")), pair), axis=0)

    partial = [
        lax.dot_general(
            half, grad_pre, (((0,), (0,)), ((), ())), preferred_element_type=F32
        ).astype(BF16)
        for half in context
    ]
    partial = jnp.stack(both(partial, core), axis=0)
    partial = partial.reshape(cores, groups, lanes, 2 * depth, width).transpose(1, 2, 0, 3, 4)
    parts = lax.all_to_all(partial.reshape(-1, depth, width), GATHER_AXES, 0, 0, tiled=True)
    weight_grad = jnp.sum(parts.astype(F32), axis=0)
    return (student_out, weight_grad)


def solution(mesh):
    groups, token_blocks, columns = (mesh.shape[name] for name in ("group", "dp", "tensor"))
    cores, xhigh, pairs = 2, 2, 2
    zhigh = groups
    fine = Mesh(
        mesh.devices.reshape(
            groups, zhigh, pairs, token_blocks // (zhigh * pairs), xhigh, columns // (xhigh * cores), cores
        ),
        ("group", "zhigh", "pair", "y", "xhigh", "xlow", "core"),
    )
    split = P(TOKEN_AXES, FEATURE_AXES)
    return jax.shard_map(
        shards,
        mesh=fine,
        in_specs=(
            split,
            P(FEATURE_AXES),
            split,
            split,
            split,
            split,
            P(FEATURE_AXES),
        ),
        out_specs=(split, split),
        check_vma=False,
    )
```

```python
import math

import jax
import jax.numpy as jnp
from jax import lax
from jax.sharding import Mesh, PartitionSpec as P

EPSILON = 1e-05
BF16 = jnp.bfloat16
F32 = jnp.float32

TOKEN_AXES = ("zhigh", "pair", "y")
GATHER_AXES = ("zhigh", "y")
FEATURE_AXES = ("group", "xhigh", "xlow", "core")
CHIP_AXES = ("xhigh", "group", "xlow")


def swap(values, axis):
    return lax.ppermute(values, axis, [(0, 1), (1, 0)])


def turned(values):
    return lax.ppermute(values, ("pair", "xhigh"), [(0, 0), (1, 2), (2, 1), (3, 3)])


def gather_features(values, after=None):
    count = lax.axis_size(CHIP_AXES)
    copies = jnp.broadcast_to(values[None], (count, *values.shape))
    line = lax.all_to_all(copies, CHIP_AXES, 0, 0, tiled=True)
    if after is not None:
        line, after = lax.optimization_barrier((line, after))
    other = swap(line, "core")
    gathered = tuple(part.reshape(2, count // 2, *values.shape) for part in (line, other))
    return gathered, after


def both(first, place):
    return (
        jnp.where(place == 0, first[0], first[1]),
        jnp.where(place == 0, first[1], first[0]),
    )


def product(parts, weight_parts, block):
    dims = (((0, 2), (0, 1)), ((), ()))
    return sum(
        lax.dot_general(part[block], weight, dims, preferred_element_type=F32)
        for part, weight in zip(parts, weight_parts)
    )


def moments(values):
    mean = jnp.mean(values, axis=1)
    centered = values - mean[:, None]
    return mean, centered, jnp.sum(centered * centered, axis=1)


def combine(means, squares, width):
    mean = jnp.mean(means, axis=0)
    shift = means - mean
    variance = jnp.mean(squares / width + shift * shift, axis=0)
    return mean, shift, lax.rsqrt(variance + EPSILON)


def gather_rows(rows):
    return lax.all_gather(jnp.stack(rows, axis=0), FEATURE_AXES, axis=0)


def shards(
    teacher_stream,
    teacher_gain,
    projection,
    student_stream,
    student_context,
    out_weight,
    student_gain,
):
    pair = lax.axis_index("pair")
    core = lax.axis_index("core")
    groups, lanes, cores = (lax.axis_size(name) for name in ("group", "xlow", "core"))
    blocks = lax.axis_size(FEATURE_AXES)
    tokens = teacher_stream.shape[0]
    token_count = tokens * lax.axis_size(TOKEN_AXES)
    width = student_stream.shape[1]
    depth = out_weight.shape[0]

    weights = jnp.concatenate([out_weight, projection], axis=0)
    zhigh = lax.axis_index("zhigh")
    weights = jnp.stack(both((weights, swap(weights, "zhigh")), zhigh), axis=0)
    context = turned(student_context)
    teacher_mean, _, teacher_square = moments(teacher_stream)
    table = gather_rows([teacher_mean, teacher_square])
    context, weights, table = lax.optimization_barrier((context, weights, table))
    weights = lax.all_gather(weights, "y", axis=0)
    mean, _, inv_std = combine(table[:, 0], table[:, 1], teacher_stream.shape[1])
    hidden = ((teacher_stream - mean[:, None]) * inv_std[:, None] * teacher_gain).astype(BF16)
    context, _ = gather_features(context)
    hidden, weights = gather_features(turned(hidden), weights)

    weights = weights.reshape(lanes, cores, 2, groups, *weights.shape[2:])
    weights = weights.transpose(1, 3, 0, 2, 4, 5)

    def weight_parts(part):
        return both(part.reshape(cores, groups * lanes, -1, width), core)

    out_full = weight_parts(weights[..., :depth, :])
    projection_full = weight_parts(weights[..., depth:, :])

    def shared(parts, weight):
        mine, other = both([product(parts, weight, block) for block in range(2)], pair)
        return mine + swap(other.astype(BF16), "pair").astype(F32)

    pre_norm = student_stream + shared(context, out_full)
    target = shared(hidden, projection_full)

    block_mean, centered, square = moments(pre_norm)
    gain_square = student_gain * student_gain
    weighted = centered * gain_square
    scaled_target = target * student_gain
    table = gather_rows(
        [
            block_mean,
            square,
            jnp.sum(weighted, axis=1),
            jnp.sum(weighted * centered, axis=1),
            jnp.sum(scaled_target, axis=1),
            jnp.sum(scaled_target * centered, axis=1),
            jnp.full((tokens,), jnp.sum(gain_square), F32),
        ]
    )
    mean, shift, inv_std = combine(table[:, 0], table[:, 1], width)
    gains = table[:, 6]
    linear = jnp.sum(table[:, 2] + shift * gains, axis=0)
    quadratic = jnp.sum(table[:, 3] + shift * (2.0 * table[:, 2] + shift * gains), axis=0)
    target_sum = jnp.sum(table[:, 4], axis=0)
    target_cross = jnp.sum(table[:, 5] + shift * table[:, 4], axis=0)
    count = width * blocks
    scale = 1.0 / math.sqrt(token_count)
    first_mean = (inv_std * linear - target_sum) * (scale / count)
    second_mean = (inv_std * inv_std * quadratic - inv_std * target_cross) * (scale / count)

    normalized = (pre_norm - mean[:, None]) * inv_std[:, None]
    student_out = normalized * student_gain
    grad_norm = (student_out - target) * scale * student_gain
    grad_pre = (
        inv_std[:, None] * (grad_norm - first_mean[:, None] - normalized * second_mean[:, None])
    ).astype(BF16)
    grads = both((grad_pre, swap(grad_pre, "pair")), pair)
    dims = (((1,), (0,)), ((), ()))
    partial = [
        sum(
            lax.dot_general(part[block], grads[block], dims, preferred_element_type=F32)
            for block in range(2)
        ).astype(BF16)
        for part in context
    ]
    partial = jnp.stack(both(partial, core), axis=0)
    partial = partial.reshape(cores, groups, lanes, 2 * depth, width).transpose(1, 2, 0, 3, 4)
    parts = lax.all_to_all(partial.reshape(-1, depth, width), GATHER_AXES, 0, 0, tiled=True)
    weight_grad = jnp.sum(parts.astype(F32), axis=0)
    return (student_out, weight_grad)


def solution(mesh):
    groups, token_blocks, columns = (mesh.shape[name] for name in ("group", "dp", "tensor"))
    cores, xhigh, pairs = 2, 2, 2
    zhigh = groups
    fine = Mesh(
        mesh.devices.reshape(
            groups, zhigh, pairs, token_blocks // (zhigh * pairs), xhigh, columns // (xhigh * cores), cores
        ),
        ("group", "zhigh", "pair", "y", "xhigh", "xlow", "core"),
    )
    split = P(TOKEN_AXES, FEATURE_AXES)
    return jax.shard_map(
        shards,
        mesh=fine,
        in_specs=(
            split,
            P(FEATURE_AXES),
            split,
            split,
            split,
            split,
            P(FEATURE_AXES),
        ),
        out_specs=(split, split),
        check_vma=False,
    )
```

```python
import math

import jax
import jax.numpy as jnp
from jax import lax
from jax.sharding import Mesh, PartitionSpec as P

EPSILON = 1e-05
BF16 = jnp.bfloat16
F32 = jnp.float32

TOKEN_AXES = ("zhigh", "pair", "y")
GATHER_AXES = ("zhigh", "y")
FEATURE_AXES = ("group", "xhigh", "xlow", "core")
CHIP_AXES = ("xhigh", "group", "xlow")


def swap(values, axis):
    return lax.ppermute(values, axis, [(0, 1), (1, 0)])


def turned(values):
    return lax.ppermute(values, ("pair", "xhigh"), [(0, 0), (1, 2), (2, 1), (3, 3)])


def spread(values):
    count = lax.axis_size(CHIP_AXES)
    copies = jnp.broadcast_to(values[None], (count, *values.shape))
    return lax.all_to_all(copies, CHIP_AXES, 0, 0, tiled=True)


def with_other_core(line):
    return tuple(
        part.reshape(2, line.shape[0] // 2, *line.shape[1:])
        for part in (line, swap(line, "core"))
    )


def both(first, place):
    return (
        jnp.where(place == 0, first[0], first[1]),
        jnp.where(place == 0, first[1], first[0]),
    )


def product(parts, weight_parts, block):
    dims = (((0, 2), (0, 1)), ((), ()))
    return sum(
        lax.dot_general(part[block], weight, dims, preferred_element_type=F32)
        for part, weight in zip(parts, weight_parts)
    )


def moments(values):
    mean = jnp.mean(values, axis=1)
    centered = values - mean[:, None]
    return mean, centered, jnp.sum(centered * centered, axis=1)


def combine(means, squares, width):
    mean = jnp.mean(means, axis=0)
    shift = means - mean
    variance = jnp.mean(squares / width + shift * shift, axis=0)
    return mean, shift, lax.rsqrt(variance + EPSILON)


def gather_rows(rows):
    return lax.all_gather(jnp.stack(rows, axis=0), FEATURE_AXES, axis=0)


def shards(
    teacher_stream,
    teacher_gain,
    projection,
    student_stream,
    student_context,
    out_weight,
    student_gain,
):
    pair = lax.axis_index("pair")
    core = lax.axis_index("core")
    groups, lanes, cores = (lax.axis_size(name) for name in ("group", "xlow", "core"))
    blocks = lax.axis_size(FEATURE_AXES)
    tokens = teacher_stream.shape[0]
    token_count = tokens * lax.axis_size(TOKEN_AXES)
    width = student_stream.shape[1]
    depth = out_weight.shape[0]

    together = lax.optimization_barrier
    weights = jnp.concatenate([out_weight, projection], axis=0)
    near = lax.all_gather(weights, "y", axis=0)
    context = turned(student_context)
    mean, _, square = moments(teacher_stream)
    context, mean, square = together((context, mean, square))
    context = spread(context)
    table = gather_rows([mean, square])
    weights, table = together((weights, table))
    far = lax.all_gather(swap(weights, "zhigh"), "y", axis=0)
    mean, _, inv_std = combine(table[:, 0], table[:, 1], teacher_stream.shape[1])
    hidden = ((teacher_stream - mean[:, None]) * inv_std[:, None] * teacher_gain).astype(BF16)
    hidden, context = together((hidden, context))
    hidden, near = together((turned(hidden), near))
    context = with_other_core(context)
    hidden, far = together((spread(hidden), far))
    hidden = with_other_core(hidden)

    weights = jnp.stack(both((near, far), lax.axis_index("zhigh")), axis=0)
    weights = weights.reshape(groups, lanes, cores, 2, *weights.shape[2:])
    weights = weights.transpose(2, 0, 1, 3, 4, 5)

    def weight_parts(part):
        return both(part.reshape(cores, groups * lanes, -1, width), core)

    out_full = weight_parts(weights[..., :depth, :])
    projection_full = weight_parts(weights[..., depth:, :])

    branch, other_branch = both([product(context, out_full, block) for block in range(2)], pair)
    target, other_target = both(
        [product(hidden, projection_full, block) for block in range(2)], pair
    )
    sent = jnp.concatenate([other_branch.astype(BF16), other_target.astype(BF16)], axis=0)
    received = swap(sent, "pair").astype(F32)
    pre_norm = student_stream + (branch + received[:tokens])
    target = target + received[tokens:]

    block_mean, centered, square = moments(pre_norm)
    gain_square = student_gain * student_gain
    weighted = centered * gain_square
    scaled_target = target * student_gain
    table = gather_rows(
        [
            block_mean,
            square,
            jnp.sum(weighted, axis=1),
            jnp.sum(weighted * centered, axis=1),
            jnp.sum(scaled_target, axis=1),
            jnp.sum(scaled_target * centered, axis=1),
            jnp.full((tokens,), jnp.sum(gain_square), F32),
        ]
    )
    mean, shift, inv_std = combine(table[:, 0], table[:, 1], width)
    gains = table[:, 6]
    linear = jnp.sum(table[:, 2] + shift * gains, axis=0)
    quadratic = jnp.sum(table[:, 3] + shift * (2.0 * table[:, 2] + shift * gains), axis=0)
    target_sum = jnp.sum(table[:, 4], axis=0)
    target_cross = jnp.sum(table[:, 5] + shift * table[:, 4], axis=0)
    count = width * blocks
    scale = 1.0 / math.sqrt(token_count)
    first_mean = (inv_std * linear - target_sum) * (scale / count)
    second_mean = (inv_std * inv_std * quadratic - inv_std * target_cross) * (scale / count)

    normalized = (pre_norm - mean[:, None]) * inv_std[:, None]
    student_out = normalized * student_gain
    grad_norm = (student_out - target) * scale * student_gain
    grad_pre = (
        inv_std[:, None] * (grad_norm - first_mean[:, None] - normalized * second_mean[:, None])
    ).astype(BF16)
    grads = both((grad_pre, swap(grad_pre, "pair")), pair)
    dims = (((1,), (0,)), ((), ()))
    partial = [
        sum(
            lax.dot_general(part[block], grads[block], dims, preferred_element_type=F32)
            for block in range(2)
        ).astype(BF16)
        for part in context
    ]
    partial = jnp.stack(both(partial, core), axis=0)
    partial = partial.reshape(cores, groups, lanes, 2 * depth, width).transpose(1, 2, 0, 3, 4)
    parts = lax.all_to_all(partial.reshape(-1, depth, width), GATHER_AXES, 0, 0, tiled=True)
    weight_grad = jnp.sum(parts.astype(F32), axis=0)
    return (student_out, weight_grad)


def solution(mesh):
    groups, token_blocks, columns = (mesh.shape[name] for name in ("group", "dp", "tensor"))
    cores, xhigh, pairs = 2, 2, 2
    zhigh = groups
    fine = Mesh(
        mesh.devices.reshape(
            groups, zhigh, pairs, token_blocks // (zhigh * pairs), xhigh, columns // (xhigh * cores), cores
        ),
        ("group", "zhigh", "pair", "y", "xhigh", "xlow", "core"),
    )
    split = P(TOKEN_AXES, FEATURE_AXES)
    return jax.shard_map(
        shards,
        mesh=fine,
        in_specs=(
            split,
            P(FEATURE_AXES),
            split,
            split,
            split,
            split,
            P(FEATURE_AXES),
        ),
        out_specs=(split, split),
        check_vma=False,
    )
```

```python
import math

import jax
import jax.numpy as jnp
from jax import lax
from jax.sharding import Mesh, PartitionSpec as P

EPSILON = 1e-05
BF16 = jnp.bfloat16
F32 = jnp.float32

TOKEN_AXES = ("zhigh", "zlow", "y")
SPLIT_AXES = ("zhigh", "zlow")
FEATURE_AXES = ("group", "xhigh", "xlow", "core")
CHIP_AXES = ("xlow", "group", "xhigh")


def turned(values):
    sizes = [lax.axis_size(name) for name in ("group", "zhigh", "zlow", "xhigh")]
    pairs = [
        (((a * sizes[1] + b) * sizes[2] + c) * sizes[3] + d, ((b * sizes[1] + a) * sizes[2] + d) * sizes[3] + c)
        for a in range(sizes[0])
        for b in range(sizes[1])
        for c in range(sizes[2])
        for d in range(sizes[3])
    ]
    return lax.ppermute(values, ("group", "zhigh", "zlow", "xhigh"), pairs)


def spread(values, axes):
    copies = jnp.broadcast_to(values[None], (lax.axis_size(axes), *values.shape))
    return lax.all_to_all(copies, axes, 0, 0, tiled=True)


def with_other_core(line):
    other = lax.ppermute(line, "core", [(0, 1), (1, 0)])
    return tuple(
        part.reshape(lax.axis_size("xlow"), -1, line.shape[2]) for part in (line, other)
    )


def both(first, place):
    return (
        jnp.where(place == 0, first[0], first[1]),
        jnp.where(place == 0, first[1], first[0]),
    )


def product(parts, weight_parts):
    dims = (((0, 2), (0, 1)), ((), ()))
    return sum(
        lax.dot_general(part, weight, dims, preferred_element_type=F32)
        for part, weight in zip(parts, weight_parts)
    )


def moments(values):
    mean = jnp.mean(values, axis=1)
    centered = values - mean[:, None]
    return mean, centered, jnp.sum(centered * centered, axis=1)


def combine(means, squares, width):
    mean = jnp.mean(means, axis=0)
    shift = means - mean
    variance = jnp.mean(squares / width + shift * shift, axis=0)
    return mean, shift, lax.rsqrt(variance + EPSILON)


def gather_rows(rows):
    return lax.all_gather(jnp.stack(rows, axis=0), FEATURE_AXES, axis=0)


def shards(
    teacher_stream,
    teacher_gain,
    projection,
    student_stream,
    student_context,
    out_weight,
    student_gain,
):
    core = lax.axis_index("core")
    place = lax.axis_index(SPLIT_AXES)
    splits = lax.axis_size(SPLIT_AXES)
    lanes, cores = (lax.axis_size(name) for name in ("xlow", "core"))
    blocks = lax.axis_size(FEATURE_AXES)
    tokens = teacher_stream.shape[0]
    token_count = tokens * lax.axis_size(TOKEN_AXES)
    width = student_stream.shape[1]
    depth = out_weight.shape[0]

    weights = lax.all_gather(jnp.concatenate([out_weight, projection], axis=0), "y", axis=0)
    together = lax.optimization_barrier
    mean, _, square = moments(teacher_stream)
    context, mean, square = together((turned(student_context), mean, square))
    table = gather_rows([mean, square])
    context, table = together((context, table))
    context = spread(context, CHIP_AXES)
    mean, _, inv_std = combine(table[:, 0], table[:, 1], teacher_stream.shape[1])
    hidden = ((teacher_stream - mean[:, None]) * inv_std[:, None] * teacher_gain).astype(BF16)
    hidden, weights = together((turned(hidden), weights))
    hidden = with_other_core(spread(hidden, CHIP_AXES))
    context = with_other_core(context)

    weights = weights.reshape(lanes, cores, 2, *weights.shape[1:]).transpose(1, 0, 2, 3, 4)

    def weight_parts(part):
        return both(part.reshape(cores, lanes, -1, width), core)

    branch = product(context, weight_parts(weights[..., :depth, :])).reshape(splits, tokens, width)
    target = product(hidden, weight_parts(weights[..., depth:, :])).reshape(splits, tokens, width)
    sent = jnp.concatenate([branch.astype(BF16), target.astype(BF16)], axis=1)
    received = lax.all_to_all(sent, SPLIT_AXES, 0, 0, tiled=True).astype(F32)

    def whole(partial, others):
        return sum(
            jnp.where(block == place, partial[block], others[block]) for block in range(splits)
        )

    pre_norm = student_stream + whole(branch, received[:, :tokens])
    target = whole(target, received[:, tokens:])

    block_mean, centered, square = moments(pre_norm)
    gain_square = student_gain * student_gain
    weighted = centered * gain_square
    scaled_target = target * student_gain
    table = gather_rows(
        [
            block_mean,
            square,
            jnp.sum(weighted, axis=1),
            jnp.sum(weighted * centered, axis=1),
            jnp.sum(scaled_target, axis=1),
            jnp.sum(scaled_target * centered, axis=1),
            jnp.full((tokens,), jnp.sum(gain_square), F32),
        ]
    )
    mean, shift, inv_std = combine(table[:, 0], table[:, 1], width)
    gains = table[:, 6]
    linear = jnp.sum(table[:, 2] + shift * gains, axis=0)
    quadratic = jnp.sum(table[:, 3] + shift * (2.0 * table[:, 2] + shift * gains), axis=0)
    target_sum = jnp.sum(table[:, 4], axis=0)
    target_cross = jnp.sum(table[:, 5] + shift * table[:, 4], axis=0)
    count = width * blocks
    scale = 1.0 / math.sqrt(token_count)
    first_mean = (inv_std * linear - target_sum) * (scale / count)
    second_mean = (inv_std * inv_std * quadratic - inv_std * target_cross) * (scale / count)

    normalized = (pre_norm - mean[:, None]) * inv_std[:, None]
    student_out = normalized * student_gain
    grad_norm = (student_out - target) * scale * student_gain
    grad_pre = (
        inv_std[:, None] * (grad_norm - first_mean[:, None] - normalized * second_mean[:, None])
    ).astype(BF16)
    grads = spread(grad_pre, SPLIT_AXES).reshape(splits * tokens, width)
    dims = (((1,), (0,)), ((), ()))
    partial = [
        lax.dot_general(part, grads, dims, preferred_element_type=F32).astype(BF16)
        for part in context
    ]
    partial = jnp.stack(both(partial, core), axis=0)
    partial = partial.reshape(cores, lanes, 2 * depth, width).transpose(1, 0, 2, 3)
    parts = lax.all_to_all(partial.reshape(-1, depth, width), "y", 0, 0, tiled=True)
    weight_grad = jnp.sum(parts.astype(F32), axis=0)
    return (student_out, weight_grad)


def solution(mesh):
    groups, token_blocks, columns = (mesh.shape[name] for name in ("group", "dp", "tensor"))
    cores, xhigh = 2, 2
    zhigh, zlow = groups, xhigh
    fine = Mesh(
        mesh.devices.reshape(
            groups, zhigh, zlow, token_blocks // (zhigh * zlow), xhigh, columns // (xhigh * cores), cores
        ),
        ("group", "zhigh", "zlow", "y", "xhigh", "xlow", "core"),
    )
    split = P(TOKEN_AXES, FEATURE_AXES)
    return jax.shard_map(
        shards,
        mesh=fine,
        in_specs=(
            split,
            P(FEATURE_AXES),
            split,
            split,
            split,
            split,
            P(FEATURE_AXES),
        ),
        out_specs=(split, split),
        check_vma=False,
    )
```

```python
import math

import jax
import jax.numpy as jnp
from jax import lax
from jax.sharding import Mesh, PartitionSpec as P

EPSILON = 1e-05
BF16 = jnp.bfloat16
F32 = jnp.float32

TOKEN_AXES = ("zhigh", "zlow", "y")
SPLIT_AXES = ("zhigh", "zlow")
FEATURE_AXES = ("group", "xhigh", "xlow", "core")
CHIP_AXES = ("xlow", "group", "xhigh")


def turned(values):
    sizes = [lax.axis_size(name) for name in ("group", "zhigh", "zlow", "xhigh")]
    pairs = [
        (((a * sizes[1] + b) * sizes[2] + c) * sizes[3] + d, ((b * sizes[1] + a) * sizes[2] + d) * sizes[3] + c)
        for a in range(sizes[0])
        for b in range(sizes[1])
        for c in range(sizes[2])
        for d in range(sizes[3])
    ]
    return lax.ppermute(values, ("group", "zhigh", "zlow", "xhigh"), pairs)


def spread(values, axes):
    copies = jnp.broadcast_to(values[None], (lax.axis_size(axes), *values.shape))
    return lax.all_to_all(copies, axes, 0, 0, tiled=True)


def group_pair(values):
    other = lax.ppermute(values, "group", [(0, 1), (1, 0)])
    return jnp.stack(both((values, other), lax.axis_index("group")), axis=0)


def ring(values):
    axes = ("xhigh", "xlow")
    count = lax.axis_size(axes)
    place = lax.axis_index(axes)
    if count == 2:
        lines = both((values, lax.ppermute(values, axes, [(0, 1), (1, 0)])), place)
    else:
        ahead = [(i, (i + 1) % count) for i in range(count)]
        back = [(i, (i - 1) % count) for i in range(count)]
        previous = lax.ppermute(values, axes, ahead)
        following = lax.ppermute(values, axes, back)
        opposite = jnp.stack(
            [lax.ppermute(previous[0], axes, ahead), lax.ppermute(following[1], axes, back)],
            axis=0,
        )
        pieces = [values, previous, opposite, following]
        lines = [lax.select_n((place - j) & (count - 1), *pieces) for j in range(count)]
    lanes = lax.axis_size("xlow")
    line = jnp.stack(
        [jnp.stack(lines[low::lanes], axis=1) for low in range(lanes)], axis=0
    )
    return line.reshape(-1, *values.shape[1:])


def scatter(parts, axes):
    count = lax.axis_size(axes)
    place = lax.axis_index(axes)
    total = sum(jnp.where(block == place, parts[block], 0.0) for block in range(count))
    sent = parts.astype(BF16)
    for step in (1, count - 1, 2):
        chunk = lax.dynamic_index_in_dim(sent, (place + step) & (count - 1), 0, keepdims=False)
        pairs = [(i, (i + step) % count) for i in range(count)]
        total = total + lax.ppermute(chunk, axes, pairs).astype(F32)
    return total


def with_other_core(line):
    other = lax.ppermute(line, "core", [(0, 1), (1, 0)])
    return tuple(
        part.reshape(lax.axis_size("xlow"), -1, line.shape[2]) for part in (line, other)
    )


def both(first, place):
    return (
        jnp.where(place == 0, first[0], first[1]),
        jnp.where(place == 0, first[1], first[0]),
    )


def product(parts, weight_parts):
    dims = (((0, 2), (0, 1)), ((), ()))
    return sum(
        lax.dot_general(part, weight, dims, preferred_element_type=F32)
        for part, weight in zip(parts, weight_parts)
    )


def moments(values):
    mean = jnp.mean(values, axis=1)
    centered = values - mean[:, None]
    return mean, centered, jnp.sum(centered * centered, axis=1)


def combine(means, squares, width):
    mean = jnp.mean(means, axis=0)
    shift = means - mean
    variance = jnp.mean(squares / width + shift * shift, axis=0)
    return mean, shift, lax.rsqrt(variance + EPSILON)


def gather_rows(rows):
    return lax.all_gather(jnp.stack(rows, axis=0), FEATURE_AXES, axis=0)


def shards(
    teacher_stream,
    teacher_gain,
    projection,
    student_stream,
    student_context,
    out_weight,
    student_gain,
):
    core = lax.axis_index("core")
    place = lax.axis_index(SPLIT_AXES)
    splits = lax.axis_size(SPLIT_AXES)
    lanes, cores = (lax.axis_size(name) for name in ("xlow", "core"))
    blocks = lax.axis_size(FEATURE_AXES)
    tokens = teacher_stream.shape[0]
    token_count = tokens * lax.axis_size(TOKEN_AXES)
    width = student_stream.shape[1]
    depth = out_weight.shape[0]

    weights = lax.all_gather(jnp.concatenate([out_weight, projection], axis=0), "y", axis=0)
    together = lax.optimization_barrier
    mean, _, square = moments(teacher_stream)
    context = group_pair(turned(student_context))
    table = gather_rows([mean, square])
    mean, _, inv_std = combine(table[:, 0], table[:, 1], teacher_stream.shape[1])
    hidden = ((teacher_stream - mean[:, None]) * inv_std[:, None] * teacher_gain).astype(BF16)
    context, hidden = together((context, turned(hidden)))
    hidden = spread(hidden, CHIP_AXES)
    context, weights = together((ring(context), weights))
    context = with_other_core(context)

    weights = weights.reshape(lanes, cores, 2, *weights.shape[1:]).transpose(1, 0, 2, 3, 4)

    def weight_parts(part):
        return both(part.reshape(cores, lanes, -1, width), core)

    branch = product(context, weight_parts(weights[..., :depth, :])).reshape(splits, tokens, width)
    hidden, _ = together((hidden, branch))
    pre_norm = student_stream + scatter(branch, SPLIT_AXES)
    hidden = with_other_core(hidden)
    target = product(hidden, weight_parts(weights[..., depth:, :])).reshape(splits, tokens, width)
    pre_norm, target = together((pre_norm, target))
    received = lax.all_to_all(target.astype(BF16), SPLIT_AXES, 0, 0, tiled=True).astype(F32)
    target = sum(
        jnp.where(block == place, target[block], received[block]) for block in range(splits)
    )

    block_mean, centered, square = moments(pre_norm)
    gain_square = student_gain * student_gain
    weighted = centered * gain_square
    scaled_target = target * student_gain
    table = gather_rows(
        [
            block_mean,
            square,
            jnp.sum(weighted, axis=1),
            jnp.sum(weighted * centered, axis=1),
            jnp.sum(scaled_target, axis=1),
            jnp.sum(scaled_target * centered, axis=1),
            jnp.full((tokens,), jnp.sum(gain_square), F32),
        ]
    )
    mean, shift, inv_std = combine(table[:, 0], table[:, 1], width)
    gains = table[:, 6]
    linear = jnp.sum(table[:, 2] + shift * gains, axis=0)
    quadratic = jnp.sum(table[:, 3] + shift * (2.0 * table[:, 2] + shift * gains), axis=0)
    target_sum = jnp.sum(table[:, 4], axis=0)
    target_cross = jnp.sum(table[:, 5] + shift * table[:, 4], axis=0)
    count = width * blocks
    scale = 1.0 / math.sqrt(token_count)
    first_mean = (inv_std * linear - target_sum) * (scale / count)
    second_mean = (inv_std * inv_std * quadratic - inv_std * target_cross) * (scale / count)

    normalized = (pre_norm - mean[:, None]) * inv_std[:, None]
    student_out = normalized * student_gain
    grad_norm = (student_out - target) * scale * student_gain
    grad_pre = (
        inv_std[:, None] * (grad_norm - first_mean[:, None] - normalized * second_mean[:, None])
    ).astype(BF16)
    grads = spread(grad_pre, SPLIT_AXES).reshape(splits * tokens, width)
    dims = (((1,), (0,)), ((), ()))
    partial = [
        lax.dot_general(part, grads, dims, preferred_element_type=F32).astype(BF16)
        for part in context
    ]
    partial = jnp.stack(both(partial, core), axis=0)
    partial = partial.reshape(cores, lanes, 2 * depth, width).transpose(1, 0, 2, 3)
    parts = lax.all_to_all(partial.reshape(-1, depth, width), "y", 0, 0, tiled=True)
    weight_grad = jnp.sum(parts.astype(F32), axis=0)
    return (student_out, weight_grad)


def solution(mesh):
    groups, token_blocks, columns = (mesh.shape[name] for name in ("group", "dp", "tensor"))
    cores, xhigh = 2, 2
    zhigh, zlow = groups, xhigh
    fine = Mesh(
        mesh.devices.reshape(
            groups, zhigh, zlow, token_blocks // (zhigh * zlow), xhigh, columns // (xhigh * cores), cores
        ),
        ("group", "zhigh", "zlow", "y", "xhigh", "xlow", "core"),
    )
    split = P(TOKEN_AXES, FEATURE_AXES)
    return jax.shard_map(
        shards,
        mesh=fine,
        in_specs=(
            split,
            P(FEATURE_AXES),
            split,
            split,
            split,
            split,
            P(FEATURE_AXES),
        ),
        out_specs=(split, split),
        check_vma=False,
    )
```

```python
import math

import jax
import jax.numpy as jnp
from jax import lax
from jax.sharding import Mesh, PartitionSpec as P

EPSILON = 1e-05
BF16 = jnp.bfloat16
F32 = jnp.float32

TOKEN_AXES = ("zhigh", "zlow", "y")
SPLIT_AXES = ("zhigh", "zlow")
FEATURE_AXES = ("group", "xhigh", "xlow", "core")
CHIP_AXES = ("xlow", "group", "xhigh")


def turned(values):
    sizes = [lax.axis_size(name) for name in ("group", "zhigh", "zlow", "xhigh")]
    pairs = [
        (((a * sizes[1] + b) * sizes[2] + c) * sizes[3] + d, ((b * sizes[1] + a) * sizes[2] + d) * sizes[3] + c)
        for a in range(sizes[0])
        for b in range(sizes[1])
        for c in range(sizes[2])
        for d in range(sizes[3])
    ]
    return lax.ppermute(values, ("group", "zhigh", "zlow", "xhigh"), pairs)


def spread(values, axes):
    copies = jnp.broadcast_to(values[None], (lax.axis_size(axes), *values.shape))
    return lax.all_to_all(copies, axes, 0, 0, tiled=True)


def with_other_core(line):
    other = lax.ppermute(line, "core", [(0, 1), (1, 0)])
    return tuple(
        part.reshape(lax.axis_size("xlow"), -1, line.shape[2]) for part in (line, other)
    )


def both(first, place):
    return (
        jnp.where(place == 0, first[0], first[1]),
        jnp.where(place == 0, first[1], first[0]),
    )


def product(parts, weight_parts):
    dims = (((0, 2), (0, 1)), ((), ()))
    return sum(
        lax.dot_general(part, weight, dims, preferred_element_type=F32)
        for part, weight in zip(parts, weight_parts)
    )


def moments(values):
    mean = jnp.mean(values, axis=1)
    centered = values - mean[:, None]
    return mean, centered, jnp.sum(centered * centered, axis=1)


def combine(means, squares, width):
    mean = jnp.mean(means, axis=0)
    shift = means - mean
    variance = jnp.mean(squares / width + shift * shift, axis=0)
    return mean, shift, lax.rsqrt(variance + EPSILON)


def gather_rows(rows):
    return lax.all_gather(jnp.stack(rows, axis=0), FEATURE_AXES, axis=0)


def shards(
    teacher_stream,
    teacher_gain,
    projection,
    student_stream,
    student_context,
    out_weight,
    student_gain,
):
    core = lax.axis_index("core")
    place = lax.axis_index(SPLIT_AXES)
    splits = lax.axis_size(SPLIT_AXES)
    lanes, cores = (lax.axis_size(name) for name in ("xlow", "core"))
    blocks = lax.axis_size(FEATURE_AXES)
    tokens = teacher_stream.shape[0]
    token_count = tokens * lax.axis_size(TOKEN_AXES)
    width = student_stream.shape[1]
    depth = out_weight.shape[0]

    weights = lax.all_gather(jnp.concatenate([out_weight, projection], axis=0), "y", axis=0)
    together = lax.optimization_barrier
    context = lax.all_gather(turned(student_context), FEATURE_AXES, axis=0)
    mean, _, square = moments(teacher_stream)
    table = gather_rows([mean, square])
    mean, _, inv_std = combine(table[:, 0], table[:, 1], teacher_stream.shape[1])
    hidden = ((teacher_stream - mean[:, None]) * inv_std[:, None] * teacher_gain).astype(BF16)
    hidden, weights = together((spread(turned(hidden), CHIP_AXES), weights))
    hidden = with_other_core(hidden)

    out_full = weights[:, :depth].reshape(lanes * cores, -1, width)
    projection_full = weights[:, depth:].reshape(lanes, cores, -1, width).transpose(1, 0, 2, 3)
    target = product(hidden, both(projection_full, core))

    def whole(partial):
        partial = partial.reshape(splits, tokens, width)
        others = lax.all_to_all(partial.astype(BF16), SPLIT_AXES, 0, 0, tiled=True).astype(F32)
        return sum(
            jnp.where(block == place, partial[block], others[block]) for block in range(splits)
        )

    target = whole(target)
    context, target = together((context, target))
    context = context.reshape(splits, lanes * cores, tokens, width).transpose(1, 0, 2, 3)
    context = context.reshape(lanes * cores, splits * tokens, width)
    pre_norm = student_stream + whole(product([context], [out_full]))

    block_mean, centered, square = moments(pre_norm)
    gain_square = student_gain * student_gain
    weighted = centered * gain_square
    scaled_target = target * student_gain
    table = gather_rows(
        [
            block_mean,
            square,
            jnp.sum(weighted, axis=1),
            jnp.sum(weighted * centered, axis=1),
            jnp.sum(scaled_target, axis=1),
            jnp.sum(scaled_target * centered, axis=1),
            jnp.full((tokens,), jnp.sum(gain_square), F32),
        ]
    )
    mean, shift, inv_std = combine(table[:, 0], table[:, 1], width)
    gains = table[:, 6]
    linear = jnp.sum(table[:, 2] + shift * gains, axis=0)
    quadratic = jnp.sum(table[:, 3] + shift * (2.0 * table[:, 2] + shift * gains), axis=0)
    target_sum = jnp.sum(table[:, 4], axis=0)
    target_cross = jnp.sum(table[:, 5] + shift * table[:, 4], axis=0)
    count = width * blocks
    scale = 1.0 / math.sqrt(token_count)
    first_mean = (inv_std * linear - target_sum) * (scale / count)
    second_mean = (inv_std * inv_std * quadratic - inv_std * target_cross) * (scale / count)

    normalized = (pre_norm - mean[:, None]) * inv_std[:, None]
    student_out = normalized * student_gain
    grad_norm = (student_out - target) * scale * student_gain
    grad_pre = (
        inv_std[:, None] * (grad_norm - first_mean[:, None] - normalized * second_mean[:, None])
    ).astype(BF16)
    grads = spread(grad_pre, SPLIT_AXES).reshape(splits * tokens, width)
    dims = (((1,), (0,)), ((), ()))
    partial = lax.dot_general(context, grads, dims, preferred_element_type=F32).astype(BF16)
    parts = lax.all_to_all(partial.reshape(-1, depth, width), "y", 0, 0, tiled=True)
    weight_grad = jnp.sum(parts.astype(F32), axis=0)
    return (student_out, weight_grad)


def solution(mesh):
    groups, token_blocks, columns = (mesh.shape[name] for name in ("group", "dp", "tensor"))
    cores, xhigh = 2, 2
    zhigh, zlow = groups, xhigh
    fine = Mesh(
        mesh.devices.reshape(
            groups, zhigh, zlow, token_blocks // (zhigh * zlow), xhigh, columns // (xhigh * cores), cores
        ),
        ("group", "zhigh", "zlow", "y", "xhigh", "xlow", "core"),
    )
    split = P(TOKEN_AXES, FEATURE_AXES)
    return jax.shard_map(
        shards,
        mesh=fine,
        in_specs=(
            split,
            P(FEATURE_AXES),
            split,
            split,
            split,
            split,
            P(FEATURE_AXES),
        ),
        out_specs=(split, split),
        check_vma=False,
    )
```

```python
import math

import jax
import jax.numpy as jnp
from jax import lax
from jax.sharding import Mesh, PartitionSpec as P

EPSILON = 1e-05
BF16 = jnp.bfloat16
F32 = jnp.float32

TOKEN_AXES = ("zhigh", "yhigh", "row")
GATHER_AXES = ("zhigh", "yhigh")
FEATURE_AXES = ("group", "x", "core")


def swap(values, axis):
    return lax.ppermute(values, axis, [(0, 1), (1, 0)])


def my_half(values, place):
    half = values.shape[1] // 2
    return (
        jnp.where(place == 0, values[:, :half], values[:, half:]),
        jnp.where(place == 0, values[:, half:], values[:, :half]),
    )


def split_tokens(values, row):
    keep, give = my_half(values, row)
    return jnp.concatenate([keep, swap(give, "row")], axis=0)


def spread(values):
    axes = ("group", "x")
    copies = jnp.broadcast_to(values[None], (lax.axis_size(axes), *values.shape))
    return lax.all_to_all(copies, axes, 0, 0, tiled=True)


def with_other_core(line):
    return tuple(
        part.transpose(1, 0, 2).reshape(line.shape[1], -1) for part in (line, swap(line, "core"))
    )


def both(first, place):
    return (
        jnp.where(place == 0, first[0], first[1]),
        jnp.where(place == 0, first[1], first[0]),
    )


def product(pair, weight_pair):
    return jnp.dot(pair[0], weight_pair[0], preferred_element_type=F32) + jnp.dot(
        pair[1], weight_pair[1], preferred_element_type=F32
    )


def moments(values):
    mean = jnp.mean(values, axis=1)
    centered = values - mean[:, None]
    return mean, centered, jnp.sum(centered * centered, axis=1)


def combine(means, squares, width):
    mean = jnp.mean(means, axis=0)
    shift = means - mean
    variance = jnp.mean(squares / width + shift * shift, axis=0)
    return mean, shift, lax.rsqrt(variance + EPSILON)


def gather_rows(rows):
    return lax.all_gather(jnp.stack(rows, axis=0), FEATURE_AXES, axis=0)


def shards(
    teacher_stream,
    teacher_gain,
    projection,
    student_stream,
    student_context,
    out_weight,
    student_gain,
):
    row = lax.axis_index("row")
    groups, lanes, cores = (lax.axis_size(name) for name in FEATURE_AXES)
    blocks = groups * lanes * cores
    tokens = teacher_stream.shape[0]
    token_count = tokens * lax.axis_size(TOKEN_AXES)
    width = student_stream.shape[1]
    depth = out_weight.shape[0]

    weights = lax.all_gather(
        jnp.concatenate([out_weight, projection], axis=0), GATHER_AXES, axis=0
    )
    weights = weights.reshape(groups, lanes, cores, *weights.shape[1:])
    weights = weights.transpose(2, 0, 1, 3, 4)
    core = lax.axis_index("core")
    out_full = both(weights[:, :, :, :depth].reshape(cores, -1, width), core)
    projection_full = both(weights[:, :, :, depth:].reshape(cores, -1, width), core)

    together = lax.optimization_barrier
    context = split_tokens(student_context, row)
    teacher_mean, _, teacher_square = moments(teacher_stream)
    table = gather_rows([teacher_mean, teacher_square])
    mean, _, inv_std = combine(table[:, 0], table[:, 1], teacher_stream.shape[1])
    hidden = ((teacher_stream - mean[:, None]) * inv_std[:, None] * teacher_gain).astype(BF16)
    hidden, context = together((spread(split_tokens(hidden, row)), context))
    hidden = with_other_core(hidden)
    target = product(hidden, projection_full)
    target = target[:tokens] + swap(target[tokens:].astype(BF16), "row").astype(F32)
    context = with_other_core(spread(context))
    branch = product(context, out_full)
    pre_norm = student_stream + (branch[:tokens] + swap(branch[tokens:].astype(BF16), "row").astype(F32))

    block_mean, centered, square = moments(pre_norm)
    gain_square = student_gain * student_gain
    weighted = centered * gain_square
    scaled_target = target * student_gain
    table = gather_rows(
        [
            block_mean,
            square,
            jnp.sum(weighted, axis=1),
            jnp.sum(weighted * centered, axis=1),
            jnp.sum(scaled_target, axis=1),
            jnp.sum(scaled_target * centered, axis=1),
            jnp.full((tokens,), jnp.sum(gain_square), F32),
        ]
    )
    mean, shift, inv_std = combine(table[:, 0], table[:, 1], width)
    gains = table[:, 6]
    linear = jnp.sum(table[:, 2] + shift * gains, axis=0)
    quadratic = jnp.sum(table[:, 3] + shift * (2.0 * table[:, 2] + shift * gains), axis=0)
    target_sum = jnp.sum(table[:, 4], axis=0)
    target_cross = jnp.sum(table[:, 5] + shift * table[:, 4], axis=0)
    count = width * blocks
    scale = 1.0 / math.sqrt(token_count)
    first_mean = (inv_std * linear - target_sum) * (scale / count)
    second_mean = (inv_std * inv_std * quadratic - inv_std * target_cross) * (scale / count)

    normalized = (pre_norm - mean[:, None]) * inv_std[:, None]
    student_out = normalized * student_gain
    grad_norm = (student_out - target) * scale * student_gain
    grad_pre = (
        inv_std[:, None] * (grad_norm - first_mean[:, None] - normalized * second_mean[:, None])
    ).astype(BF16)
    grad_pre = jnp.concatenate([grad_pre, swap(grad_pre, "row")], axis=0)

    partial = [
        lax.dot_general(
            half, grad_pre, (((0,), (0,)), ((), ())), preferred_element_type=F32
        ).astype(BF16)
        for half in context
    ]
    partial = jnp.stack(both(partial, core), axis=0)
    partial = partial.reshape(cores, groups, lanes, depth, width).transpose(1, 2, 0, 3, 4)
    parts = lax.all_to_all(partial.reshape(blocks, depth, width), GATHER_AXES, 0, 0, tiled=True)
    weight_grad = jnp.sum(parts.astype(F32), axis=0)
    return (student_out, weight_grad)


def solution(mesh):
    groups, token_blocks, columns = (mesh.shape[name] for name in ("group", "dp", "tensor"))
    cores = 2
    zhigh = min(4, token_blocks // 4)
    fine = Mesh(
        mesh.devices.reshape(
            groups, zhigh, token_blocks // (2 * zhigh), 2, columns // cores, cores
        ),
        ("group", "zhigh", "yhigh", "row", "x", "core"),
    )
    split = P(TOKEN_AXES, FEATURE_AXES)
    return jax.shard_map(
        shards,
        mesh=fine,
        in_specs=(
            split,
            P(FEATURE_AXES),
            split,
            split,
            split,
            split,
            P(FEATURE_AXES),
        ),
        out_specs=(split, split),
        check_vma=False,
    )
```

```python
import math

import jax
import jax.numpy as jnp
from jax import lax
from jax.sharding import Mesh, PartitionSpec as P

EPSILON = 1e-05
BF16 = jnp.bfloat16
F32 = jnp.float32

TOKEN_AXES = ("zhigh", "yhigh", "row")
GATHER_AXES = ("zhigh", "yhigh")
FEATURE_AXES = ("group", "x", "core")


def swap(values, axis):
    return lax.ppermute(values, axis, [(0, 1), (1, 0)])


def my_half(values, place):
    half = values.shape[1] // 2
    return (
        jnp.where(place == 0, values[:, :half], values[:, half:]),
        jnp.where(place == 0, values[:, half:], values[:, :half]),
    )


def split_tokens(values, row):
    keep, give = my_half(values, row)
    return jnp.concatenate([keep, swap(give, "row")], axis=0)


def gather_features(values):
    axes = ("group", "x")
    count = lax.axis_size(axes)
    copies = jnp.broadcast_to(values[None], (count, *values.shape))
    line = lax.all_to_all(copies, axes, 0, 0, tiled=True)
    other = swap(line, "core")
    return tuple(
        part.transpose(1, 0, 2).reshape(values.shape[0], -1) for part in (line, other)
    )


def both(first, place):
    return (
        jnp.where(place == 0, first[0], first[1]),
        jnp.where(place == 0, first[1], first[0]),
    )


def product(pair, weight_pair):
    return jnp.dot(pair[0], weight_pair[0], preferred_element_type=F32) + jnp.dot(
        pair[1], weight_pair[1], preferred_element_type=F32
    )


def moments(values):
    mean = jnp.mean(values, axis=1)
    centered = values - mean[:, None]
    return mean, centered, jnp.sum(centered * centered, axis=1)


def combine(means, squares, width):
    mean = jnp.mean(means, axis=0)
    shift = means - mean
    variance = jnp.mean(squares / width + shift * shift, axis=0)
    return mean, shift, lax.rsqrt(variance + EPSILON)


def gather_rows(rows):
    return lax.all_gather(jnp.stack(rows, axis=0), FEATURE_AXES, axis=0)


def shards(
    teacher_stream,
    teacher_gain,
    projection,
    student_stream,
    student_context,
    out_weight,
    student_gain,
):
    row = lax.axis_index("row")
    groups, lanes, cores = (lax.axis_size(name) for name in FEATURE_AXES)
    blocks = groups * lanes * cores
    tokens = teacher_stream.shape[0]
    token_count = tokens * lax.axis_size(TOKEN_AXES)
    width = student_stream.shape[1]
    depth = out_weight.shape[0]

    weights = lax.all_gather(
        jnp.concatenate([out_weight, projection], axis=0), GATHER_AXES, axis=0
    )
    weights = weights.reshape(groups, lanes, cores, *weights.shape[1:])
    weights = weights.transpose(2, 0, 1, 3, 4)
    core = lax.axis_index("core")
    out_full = both(weights[:, :, :, :depth].reshape(cores, -1, width), core)
    projection_full = both(weights[:, :, :, depth:].reshape(cores, -1, width), core)

    context = gather_features(split_tokens(student_context, row))

    teacher_mean, _, teacher_square = moments(teacher_stream)
    table = gather_rows([teacher_mean, teacher_square])
    mean, _, inv_std = combine(table[:, 0], table[:, 1], teacher_stream.shape[1])
    hidden = ((teacher_stream - mean[:, None]) * inv_std[:, None] * teacher_gain).astype(BF16)
    hidden = gather_features(split_tokens(hidden, row))

    branch = product(context, out_full)
    pre_norm = student_stream + (branch[:tokens] + swap(branch[tokens:].astype(BF16), "row").astype(F32))
    target = product(hidden, projection_full)
    target = target[:tokens] + swap(target[tokens:].astype(BF16), "row").astype(F32)

    block_mean, centered, square = moments(pre_norm)
    gain_square = student_gain * student_gain
    weighted = centered * gain_square
    scaled_target = target * student_gain
    table = gather_rows(
        [
            block_mean,
            square,
            jnp.sum(weighted, axis=1),
            jnp.sum(weighted * centered, axis=1),
            jnp.sum(scaled_target, axis=1),
            jnp.sum(scaled_target * centered, axis=1),
            jnp.full((tokens,), jnp.sum(gain_square), F32),
        ]
    )
    mean, shift, inv_std = combine(table[:, 0], table[:, 1], width)
    gains = table[:, 6]
    linear = jnp.sum(table[:, 2] + shift * gains, axis=0)
    quadratic = jnp.sum(table[:, 3] + shift * (2.0 * table[:, 2] + shift * gains), axis=0)
    target_sum = jnp.sum(table[:, 4], axis=0)
    target_cross = jnp.sum(table[:, 5] + shift * table[:, 4], axis=0)
    count = width * blocks
    scale = 1.0 / math.sqrt(token_count)
    first_mean = (inv_std * linear - target_sum) * (scale / count)
    second_mean = (inv_std * inv_std * quadratic - inv_std * target_cross) * (scale / count)

    normalized = (pre_norm - mean[:, None]) * inv_std[:, None]
    student_out = normalized * student_gain
    grad_norm = (student_out - target) * scale * student_gain
    grad_pre = (
        inv_std[:, None] * (grad_norm - first_mean[:, None] - normalized * second_mean[:, None])
    ).astype(BF16)
    grad_pre = jnp.concatenate([grad_pre, swap(grad_pre, "row")], axis=0)

    partial = [
        lax.dot_general(
            half, grad_pre, (((0,), (0,)), ((), ())), preferred_element_type=F32
        ).astype(BF16)
        for half in context
    ]
    partial = jnp.stack(both(partial, core), axis=0)
    partial = partial.reshape(cores, groups, lanes, depth, width).transpose(1, 2, 0, 3, 4)
    partial = partial.reshape(lax.axis_size("zhigh"), lax.axis_size("yhigh"), depth, width)
    parts = lax.all_to_all(partial.transpose(1, 0, 2, 3), "yhigh", 0, 0, tiled=True)
    parts = lax.all_to_all(jnp.sum(parts.astype(F32), axis=0), "zhigh", 0, 0, tiled=True)
    weight_grad = jnp.sum(parts, axis=0)
    return (student_out, weight_grad)


def solution(mesh):
    groups, token_blocks, columns = (mesh.shape[name] for name in ("group", "dp", "tensor"))
    cores = 2
    zhigh = min(4, token_blocks // 4)
    fine = Mesh(
        mesh.devices.reshape(
            groups, zhigh, token_blocks // (2 * zhigh), 2, columns // cores, cores
        ),
        ("group", "zhigh", "yhigh", "row", "x", "core"),
    )
    split = P(TOKEN_AXES, FEATURE_AXES)
    return jax.shard_map(
        shards,
        mesh=fine,
        in_specs=(
            split,
            P(FEATURE_AXES),
            split,
            split,
            split,
            split,
            P(FEATURE_AXES),
        ),
        out_specs=(split, split),
        check_vma=False,
    )
```

```python
import math

import jax
import jax.numpy as jnp
from jax import lax
from jax.sharding import Mesh, PartitionSpec as P

EPSILON = 1e-05
BF16 = jnp.bfloat16
F32 = jnp.float32

TOKEN_AXES = ("zhigh", "yhigh", "row")
GATHER_AXES = ("zhigh", "yhigh")
FEATURE_AXES = ("group", "x", "core")


def swap(values, axis):
    return lax.ppermute(values, axis, [(0, 1), (1, 0)])


def my_half(values, place):
    half = values.shape[1] // 2
    return (
        jnp.where(place == 0, values[:, :half], values[:, half:]),
        jnp.where(place == 0, values[:, half:], values[:, :half]),
    )


def split_tokens(values, row):
    keep, give = my_half(values, row)
    return jnp.concatenate([keep, swap(give, "row")], axis=0)


def gather_features(values):
    axes = ("group", "x")
    count = lax.axis_size(axes)
    copies = jnp.broadcast_to(values[None], (count, *values.shape))
    line = lax.all_to_all(copies, axes, 0, 0, tiled=True)
    other = swap(line, "core")
    return tuple(
        part.transpose(1, 0, 2).reshape(values.shape[0], -1) for part in (line, other)
    )


def both(first, place):
    return (
        jnp.where(place == 0, first[0], first[1]),
        jnp.where(place == 0, first[1], first[0]),
    )


def product(pair, weight_pair):
    return jnp.dot(pair[0], weight_pair[0], preferred_element_type=F32) + jnp.dot(
        pair[1], weight_pair[1], preferred_element_type=F32
    )


def moments(values):
    mean = jnp.mean(values, axis=1)
    centered = values - mean[:, None]
    return mean, centered, jnp.sum(centered * centered, axis=1)


def combine(means, squares, width):
    mean = jnp.mean(means, axis=0)
    shift = means - mean
    variance = jnp.mean(squares / width + shift * shift, axis=0)
    return mean, shift, lax.rsqrt(variance + EPSILON)


def gather_rows(rows):
    return lax.all_gather(jnp.stack(rows, axis=0), FEATURE_AXES, axis=0)


def shards(
    teacher_stream,
    teacher_gain,
    projection,
    student_stream,
    student_context,
    out_weight,
    student_gain,
):
    row = lax.axis_index("row")
    groups, lanes, cores = (lax.axis_size(name) for name in FEATURE_AXES)
    blocks = groups * lanes * cores
    tokens = teacher_stream.shape[0]
    token_count = tokens * lax.axis_size(TOKEN_AXES)
    width = student_stream.shape[1]
    depth = out_weight.shape[0]

    weights = lax.all_gather(
        jnp.concatenate([out_weight, projection], axis=0), GATHER_AXES, axis=0
    )
    weights = weights.reshape(groups, lanes, cores, *weights.shape[1:])
    weights = weights.transpose(2, 0, 1, 3, 4)
    core = lax.axis_index("core")
    out_full = both(weights[:, :, :, :depth].reshape(cores, -1, width), core)
    projection_full = both(weights[:, :, :, depth:].reshape(cores, -1, width), core)

    context = gather_features(split_tokens(student_context, row))

    teacher_mean, _, teacher_square = moments(teacher_stream)
    table = gather_rows([teacher_mean, teacher_square])
    mean, _, inv_std = combine(table[:, 0], table[:, 1], teacher_stream.shape[1])
    hidden = ((teacher_stream - mean[:, None]) * inv_std[:, None] * teacher_gain).astype(BF16)
    hidden = gather_features(split_tokens(hidden, row))

    branch = product(context, out_full)
    target = product(hidden, projection_full)
    sent = jnp.concatenate([branch[tokens:].astype(BF16), target[tokens:].astype(BF16)], axis=0)
    received = swap(sent, "row").astype(F32)
    pre_norm = student_stream + (branch[:tokens] + received[:tokens])
    target = target[:tokens] + received[tokens:]

    block_mean, centered, square = moments(pre_norm)
    gain_square = student_gain * student_gain
    weighted = centered * gain_square
    scaled_target = target * student_gain
    table = gather_rows(
        [
            block_mean,
            square,
            jnp.sum(weighted, axis=1),
            jnp.sum(weighted * centered, axis=1),
            jnp.sum(scaled_target, axis=1),
            jnp.sum(scaled_target * centered, axis=1),
            jnp.full((tokens,), jnp.sum(gain_square), F32),
        ]
    )
    mean, shift, inv_std = combine(table[:, 0], table[:, 1], width)
    gains = table[:, 6]
    linear = jnp.sum(table[:, 2] + shift * gains, axis=0)
    quadratic = jnp.sum(table[:, 3] + shift * (2.0 * table[:, 2] + shift * gains), axis=0)
    target_sum = jnp.sum(table[:, 4], axis=0)
    target_cross = jnp.sum(table[:, 5] + shift * table[:, 4], axis=0)
    count = width * blocks
    scale = 1.0 / math.sqrt(token_count)
    first_mean = (inv_std * linear - target_sum) * (scale / count)
    second_mean = (inv_std * inv_std * quadratic - inv_std * target_cross) * (scale / count)

    normalized = (pre_norm - mean[:, None]) * inv_std[:, None]
    student_out = normalized * student_gain
    grad_norm = (student_out - target) * scale * student_gain
    grad_pre = (
        inv_std[:, None] * (grad_norm - first_mean[:, None] - normalized * second_mean[:, None])
    ).astype(BF16)
    grad_pre = jnp.concatenate([grad_pre, swap(grad_pre, "row")], axis=0)

    partial = [
        lax.dot_general(
            half, grad_pre, (((0,), (0,)), ((), ())), preferred_element_type=F32
        ).astype(BF16)
        for half in context
    ]
    partial = jnp.stack(both(partial, core), axis=0)
    partial = partial.reshape(cores, groups, lanes, depth, width).transpose(1, 2, 0, 3, 4)
    parts = lax.all_to_all(partial.reshape(blocks, depth, width), GATHER_AXES, 0, 0, tiled=True)
    weight_grad = jnp.sum(parts.astype(F32), axis=0)
    return (student_out, weight_grad)


def solution(mesh):
    groups, token_blocks, columns = (mesh.shape[name] for name in ("group", "dp", "tensor"))
    cores = 2
    zhigh = min(4, token_blocks // 4)
    fine = Mesh(
        mesh.devices.reshape(
            groups, zhigh, token_blocks // (2 * zhigh), 2, columns // cores, cores
        ),
        ("group", "zhigh", "yhigh", "row", "x", "core"),
    )
    split = P(TOKEN_AXES, FEATURE_AXES)
    return jax.shard_map(
        shards,
        mesh=fine,
        in_specs=(
            split,
            P(FEATURE_AXES),
            split,
            split,
            split,
            split,
            P(FEATURE_AXES),
        ),
        out_specs=(split, split),
        check_vma=False,
    )
```
